512 devices in a mesh: ri: 16 (over z_hi, x), rj: 32 (over z_lo, y, core).
Axes of the slice: x: 4, y: 4, z: 16 (z_hi: 4, z_lo: 4; z = z_hi * 4 + z_lo), core: 2. Of those that a mesh axis runs over, the one named last changes fastest.
Arguments:
- couple_sensitivity: bfloat16 [512, 512, 128], P('ri', 'rj'), may hold values from -6 to 6
- stored_first_halves: bfloat16 [512, 4096], P('ri', 'rj'), may hold values from -6 to 6
- stored_second_halves: bfloat16 [512, 4096], P('ri', 'rj'), may hold values from -6 to 6
- incoming_sensitivity: bfloat16 [512, 128, 256], P('ri', 'rj'), may hold values from -6 to 6
- homolog_activations: bfloat16 [512, 128, 256], P('ri', 'rj'), may hold values from -4 to 4
- tensor_couple_map: bfloat16 [1024, 128], replicated, may hold values from -0.5 to 0.5
- homolog_to_half_map: bfloat16 [256, 64], replicated, may hold values from -0.75 to 0.75
- query_key_value_gate_map: bfloat16 [256, 1024], replicated, may hold values from -0.375 to 0.375
- attended_result_map: bfloat16 [256, 256], replicated, may hold values from -0.75 to 0.75
Outputs:
- msa_grad_out: bfloat16 [512, 128, 256], P('ri', 'rj')
The draws below stay inside these ranges and needn't reach their ends.
All inputs are finite; a program needn't handle non-finite values.
Results may differ from the reference program's by a relative error of at most 0.009.
Values may be sent and summed in bfloat16 or wider, within the bound.
No kernel may reach another device: no remote copies, remote signals or barrier semaphores. Data moves between devices by JAX's collectives and lax.ppermute only.
A program may use at most 64 MiB of HBM per device.

```python
import jax
import jax.numpy as jnp
from jax import lax

HOMOLOG_FEATURES = 256
CZ = 128
HALF_FEATURES = 32
HEADS = 8
SEQ_HOMOLOGS = 128
WINDOW_AMINO = 512


def block_scale(key, extent, cuts, least, high):
    level, own = 1.0, jax.random.fold_in(key, 6)
    for position, parts in cuts:
        steps = jnp.exp(jax.random.uniform(jax.random.fold_in(own, position), (parts,), jnp.float32, least / len(cuts), high / len(cuts)))
        level = level * jnp.repeat(steps, extent[position] // parts).reshape([-1 if axis == position else 1 for axis in range(len(extent))])
    return level


def scatter_about(own_key, extent, deviation, bound, shards=(), dtype=jnp.bfloat16):
    values = jax.random.normal(own_key, extent, jnp.float32) * deviation
    if len(shards) > 0:
        values = block_scale(own_key, extent, shards, -0.22, 0.18) * values
    return jnp.clip(values, min=-bound, max=bound).astype(dtype)


def setup_inputs(seed: int = 0) -> dict:
    arg_keys = jax.random.split(jax.random.key(seed), 10)
    couple_sensitivity = scatter_about(arg_keys[0], (WINDOW_AMINO, WINDOW_AMINO, CZ), 1.0, 6.0, ((0, 16), (1, 32)))
    stored_first_halves = scatter_about(arg_keys[1], (WINDOW_AMINO, SEQ_HOMOLOGS * HALF_FEATURES), 1.0, 6.0, ((0, 16), (1, 32)))
    stored_second_halves = scatter_about(arg_keys[2], (WINDOW_AMINO, SEQ_HOMOLOGS * HALF_FEATURES), 1.0, 6.0, ((0, 16), (1, 32)))
    incoming_sensitivity = scatter_about(arg_keys[3], (WINDOW_AMINO, SEQ_HOMOLOGS, HOMOLOG_FEATURES), 1.0, 6.0, ((0, 16), (1, 32)))
    homolog_activations = scatter_about(arg_keys[4], (WINDOW_AMINO, SEQ_HOMOLOGS, HOMOLOG_FEATURES), 1.0, 4.0, ((0, 16), (1, 32)))
    tensor_couple_map = scatter_about(arg_keys[5], (HALF_FEATURES * HALF_FEATURES, CZ), CZ ** -0.5, 0.5)
    homolog_to_half_map = scatter_about(arg_keys[6], (HOMOLOG_FEATURES, 2 * HALF_FEATURES), (2 * HALF_FEATURES) ** -0.5, 0.75)
    query_key_value_gate_map = scatter_about(arg_keys[7], (HOMOLOG_FEATURES, 4 * HOMOLOG_FEATURES), HOMOLOG_FEATURES ** -0.5, 0.375)
    attended_result_map = scatter_about(arg_keys[8], (HOMOLOG_FEATURES, HOMOLOG_FEATURES), (HOMOLOG_FEATURES // 4) ** -0.5, 0.75)
    return {"couple_sensitivity": couple_sensitivity, "stored_first_halves": stored_first_halves, "stored_second_halves": stored_second_halves, "incoming_sensitivity": incoming_sensitivity, "homolog_activations": homolog_activations, "tensor_couple_map": tensor_couple_map, "homolog_to_half_map": homolog_to_half_map, "query_key_value_gate_map": query_key_value_gate_map, "attended_result_map": attended_result_map}


def matrix_product(form, first, second):
    return jnp.einsum(form, first.astype(jnp.float32), second.astype(jnp.float32))


def rounded_length(values_in):
    return lax.optimization_barrier(values_in.astype(jnp.bfloat16))


def column_attention_backward(alignment_block, block_gradient, query_key_value_gate_map, attended_result_map):
    amino_number, sequence_depth_rows, feature_number = alignment_block.shape
    head_size = feature_number // HEADS
    score_scale = head_size ** -0.5
    projected_factors = rounded_length(matrix_product('tcx,xy->tcy', alignment_block, query_key_value_gate_map))
    shaped = projected_factors.reshape(amino_number, sequence_depth_rows, 4, HEADS, head_size)
    queries = shaped[:, :, 0]
    key_heads = shaped[:, :, 1]
    values = shaped[:, :, 2]
    gate_logits = shaped[:, :, 3]
    scores = matrix_product('nshd,nthd->nhst', queries, key_heads) * score_scale
    weights = jnp.exp(scores)
    attention = weights / jnp.sum(weights, axis=-1, keepdims=True)
    attention_low = rounded_length(attention)
    attended = matrix_product('nhst,nthd->nshd', attention_low, values)
    gate_open = jax.nn.sigmoid(gate_logits.astype(jnp.float32))
    grad_gated = matrix_product('nsm,om->nso', block_gradient, attended_result_map).reshape(amino_number, sequence_depth_rows, HEADS, head_size)
    grad_attended = rounded_length(gate_open * grad_gated)
    grad_logits = grad_gated * attended * gate_open * (1.0 - gate_open)
    grad_weights = matrix_product('nshd,nthd->nhst', grad_attended, values)
    grad_scores = rounded_length(attention * (grad_weights - jnp.sum(attention * grad_weights, axis=-1, keepdims=True)) * score_scale)
    grad_queries = matrix_product('nhst,nthd->nshd', grad_scores, key_heads)
    grad_keys = matrix_product('nhst,nshd->nthd', grad_scores, queries)
    grad_values = matrix_product('nhst,nshd->nthd', attention_low, grad_attended)
    projection_gradient = rounded_length(jnp.stack([grad_queries, grad_keys, grad_values, grad_logits], axis=2).reshape(amino_number, sequence_depth_rows, 4 * feature_number))
    alignment_gradient = matrix_product('eia,qa->eiq', projection_gradient, query_key_value_gate_map)
    return (block_gradient.astype(jnp.float32) + alignment_gradient).astype(jnp.bfloat16)


def reference(couple_sensitivity, stored_first_halves, stored_second_halves, incoming_sensitivity, homolog_activations, tensor_couple_map, homolog_to_half_map, query_key_value_gate_map, attended_result_map):
    amino_number = couple_sensitivity.shape[0]
    left_reshaped = stored_first_halves.reshape(amino_number, SEQ_HOMOLOGS, HALF_FEATURES)
    right_reshaped = stored_second_halves.reshape(amino_number, SEQ_HOMOLOGS, HALF_FEATURES)
    block_list = amino_number // 16
    pair_block_list = couple_sensitivity.reshape(block_list, 16, amino_number, CZ)
    left_block_list = left_reshaped.reshape(block_list, 16, SEQ_HOMOLOGS, HALF_FEATURES)

    def step_forward(loop_state, pieces):
        pair_piece, left_portion = pieces
        outer_product = rounded_length(matrix_product('ijk,fk->ijf', pair_piece, tensor_couple_map)).reshape(16, amino_number, HALF_FEATURES, HALF_FEATURES)
        left_portion_gradient = matrix_product('altg,lbg->abt', outer_product, right_reshaped) / SEQ_HOMOLOGS
        loop_state = loop_state + matrix_product('lzno,lwn->zwo', outer_product, left_portion) / SEQ_HOMOLOGS
        return loop_state, left_portion_gradient

    right_gradient, left_stacked = lax.scan(step_forward, jnp.zeros((amino_number, SEQ_HOMOLOGS, HALF_FEATURES), jnp.float32), (pair_block_list, left_block_list))
    left_gradient = left_stacked.reshape(amino_number, SEQ_HOMOLOGS, HALF_FEATURES)
    factor_gradient = rounded_length(jnp.concatenate([left_gradient, right_gradient], axis=-1))
    alignment_grad_total = rounded_length(incoming_sensitivity.astype(jnp.float32) + matrix_product('whb,ib->whi', factor_gradient, homolog_to_half_map))
    feature_number = homolog_activations.shape[2]
    homolog_pieces = homolog_activations.reshape(amino_number // 16, 16, SEQ_HOMOLOGS, feature_number)
    gradient_parts = alignment_grad_total.reshape(amino_number // 16, 16, SEQ_HOMOLOGS, feature_number)

    def column_slab(pieces):
        return column_attention_backward(pieces[0], pieces[1], query_key_value_gate_map, attended_result_map)

    final_output = lax.map(column_slab, (homolog_pieces, gradient_parts))
    return final_output.reshape(amino_number, SEQ_HOMOLOGS, feature_number)
```

```python
import jax
import jax.numpy as jnp
from jax import lax
from jax.sharding import PartitionSpec as P

HALF = 32
HEADS = 8


def attention_backward(acts, grad, qkvg_map, result_map):
    rows, features = acts.shape
    head = features // HEADS
    scale = head ** (-0.5)
    projected = jnp.einsum(
        "cx,xy->cy", acts, qkvg_map, preferred_element_type=jnp.float32
    ).astype(jnp.bfloat16)
    shaped = projected.reshape(rows, 4, HEADS, head)
    queries, keys, values, logits = shaped[:, 0], shaped[:, 1], shaped[:, 2], shaped[:, 3]
    scores = jnp.einsum("shd,thd->hst", queries, keys, preferred_element_type=jnp.float32) * scale
    weights = jnp.exp(scores)
    attention = weights / jnp.sum(weights, axis=-1, keepdims=True)
    low = attention.astype(jnp.bfloat16)
    attended = jnp.einsum("hst,thd->shd", low, values, preferred_element_type=jnp.float32)
    gate = jax.nn.sigmoid(logits.astype(jnp.float32))
    grad_gated = jnp.einsum(
        "sm,om->so", grad, result_map, preferred_element_type=jnp.float32
    ).reshape(rows, HEADS, head)
    grad_attended = (gate * grad_gated).astype(jnp.bfloat16)
    grad_logits = grad_gated * attended * gate * (1.0 - gate)
    grad_weights = jnp.einsum(
        "shd,thd->hst", grad_attended, values, preferred_element_type=jnp.float32
    )
    grad_scores = (
        attention
        * (grad_weights - jnp.sum(attention * grad_weights, axis=-1, keepdims=True))
        * scale
    ).astype(jnp.bfloat16)
    grad_queries = jnp.einsum("hst,thd->shd", grad_scores, keys, preferred_element_type=jnp.float32)
    grad_keys = jnp.einsum("hst,shd->thd", grad_scores, queries, preferred_element_type=jnp.float32)
    grad_values = jnp.einsum("hst,shd->thd", low, grad_attended, preferred_element_type=jnp.float32)
    grad_projected = (
        jnp.stack([grad_queries, grad_keys, grad_values, grad_logits], axis=1)
        .reshape(rows, 4 * features)
        .astype(jnp.bfloat16)
    )
    back = jnp.einsum("sa,qa->sq", grad_projected, qkvg_map, preferred_element_type=jnp.float32)
    return (grad.astype(jnp.float32) + back).astype(jnp.bfloat16)


def local(
    pair,
    first,
    second,
    incoming,
    acts,
    couple_map,
    half_map,
    qkvg_map,
    result_map,
):
    ni = lax.axis_size("ri")
    nj = lax.axis_size("rj")
    q = lax.axis_index("rj")
    rows, cols, pair_features = pair.shape
    own_rows = incoming.shape[1]
    depth = own_rows * nj
    features = incoming.shape[2]

    acts_res = lax.all_to_all(acts, "rj", split_axis=0, concat_axis=1, tiled=True)
    inc_res = lax.all_to_all(incoming, "rj", split_axis=0, concat_axis=1, tiled=True)

    left = lax.all_to_all(
        jnp.broadcast_to(first[None], (nj,) + first.shape), "rj", 0, 0, tiled=True
    ).reshape(nj, rows, own_rows, HALF)

    received = []
    for k in range(2):
        piece = lax.dynamic_slice_in_dim(second, (q + k) % 2 * cols, cols, 0)
        perm = [
            (a * nj + b, (b // 2) * nj + 2 * a + (b + k) % 2) for a in range(ni) for b in range(nj)
        ]
        received.append(lax.ppermute(piece, ("ri", "rj"), perm))
    even = q % 2 == 0
    right = jnp.stack(
        [
            jnp.where(even, received[0], received[1]),
            jnp.where(even, received[1], received[0]),
        ]
    )
    right = lax.all_to_all(
        jnp.broadcast_to(right[None], (ni,) + right.shape), "ri", 0, 0, tiled=True
    ).reshape(nj, cols, own_rows, HALF)

    outer = jnp.einsum(
        "ijk,cek->icje",
        pair,
        couple_map.reshape(HALF, HALF, pair_features),
        preferred_element_type=jnp.float32,
    ).astype(jnp.bfloat16)
    left_t = left.transpose(1, 3, 0, 2).reshape(rows, HALF, depth)
    right_t = right.transpose(1, 3, 0, 2).reshape(cols, HALF, depth)
    right_part = jnp.einsum("icje,ics->jes", outer, left_t, preferred_element_type=jnp.float32)
    right_part = (right_part / depth).astype(jnp.bfloat16)
    right_sent = lax.all_to_all(right_part, "ri", 0, 0, tiled=True)
    left_part = jnp.einsum("icje,jes->ics", outer, right_t, preferred_element_type=jnp.float32)
    left_part = (left_part / depth).astype(jnp.bfloat16)
    left_sent = lax.all_to_all(left_part, "rj", 0, 0, tiled=True)
    right_grad = jnp.sum(right_sent.astype(jnp.float32), axis=0).astype(jnp.bfloat16)
    perm = [
        (a * nj + b, (b // 2) * nj + (b % 2) * cols + a) for a in range(ni) for b in range(nj)
    ]
    right_grad = lax.ppermute(right_grad, ("ri", "rj"), perm)
    left_grad = jnp.sum(left_sent.astype(jnp.float32), axis=0).astype(jnp.bfloat16)
    factor = jnp.concatenate([left_grad, right_grad], axis=0)
    grad = (
        inc_res[0].astype(jnp.float32)
        + jnp.einsum("fs,mf->sm", factor, half_map, preferred_element_type=jnp.float32)
    ).astype(jnp.bfloat16)
    result = attention_backward(acts_res[0], grad, qkvg_map, result_map)
    return lax.all_to_all(result[None], "rj", split_axis=1, concat_axis=0, tiled=True)


def solution(mesh):
    return jax.shard_map(
        local,
        mesh=mesh,
        in_specs=(
            P("ri", "rj", None),
            P("ri", "rj"),
            P("ri", "rj"),
            P("ri", "rj", None),
            P("ri", "rj", None),
            P(),
            P(),
            P(),
            P(),
        ),
        out_specs=P("ri", "rj", None),
        check_vma=False,
    )
```

```python
import jax
import jax.numpy as jnp
from jax import lax
from jax.sharding import PartitionSpec as P

HALF = 32
HEADS = 8


def attention_backward(acts, grad, qkvg_map, result_map):
    rows, features = acts.shape
    head = features // HEADS
    scale = head ** (-0.5)
    projected = jnp.einsum(
        "cx,xy->cy", acts, qkvg_map, preferred_element_type=jnp.float32
    ).astype(jnp.bfloat16)
    shaped = projected.reshape(rows, 4, HEADS, head)
    queries, keys, values, logits = shaped[:, 0], shaped[:, 1], shaped[:, 2], shaped[:, 3]
    scores = jnp.einsum("shd,thd->hst", queries, keys, preferred_element_type=jnp.float32) * scale
    weights = jnp.exp(scores)
    attention = weights / jnp.sum(weights, axis=-1, keepdims=True)
    low = attention.astype(jnp.bfloat16)
    attended = jnp.einsum("hst,thd->shd", low, values, preferred_element_type=jnp.float32)
    gate = jax.nn.sigmoid(logits.astype(jnp.float32))
    grad_gated = jnp.einsum(
        "sm,om->so", grad, result_map, preferred_element_type=jnp.float32
    ).reshape(rows, HEADS, head)
    grad_attended = (gate * grad_gated).astype(jnp.bfloat16)
    grad_logits = grad_gated * attended * gate * (1.0 - gate)
    grad_weights = jnp.einsum(
        "shd,thd->hst", grad_attended, values, preferred_element_type=jnp.float32
    )
    grad_scores = (
        attention
        * (grad_weights - jnp.sum(attention * grad_weights, axis=-1, keepdims=True))
        * scale
    ).astype(jnp.bfloat16)
    grad_queries = jnp.einsum("hst,thd->shd", grad_scores, keys, preferred_element_type=jnp.float32)
    grad_keys = jnp.einsum("hst,shd->thd", grad_scores, queries, preferred_element_type=jnp.float32)
    grad_values = jnp.einsum("hst,shd->thd", low, grad_attended, preferred_element_type=jnp.float32)
    grad_projected = (
        jnp.stack([grad_queries, grad_keys, grad_values, grad_logits], axis=1)
        .reshape(rows, 4 * features)
        .astype(jnp.bfloat16)
    )
    back = jnp.einsum("sa,qa->sq", grad_projected, qkvg_map, preferred_element_type=jnp.float32)
    return (grad.astype(jnp.float32) + back).astype(jnp.bfloat16)


def local(
    pair,
    first,
    second,
    incoming,
    acts,
    couple_map,
    half_map,
    qkvg_map,
    result_map,
):
    ni = lax.axis_size("ri")
    nj = lax.axis_size("rj")
    chips = nj // 2
    core = lax.axis_index("rj") % 2
    rows, cols, pair_features = pair.shape
    own_rows = incoming.shape[1]
    depth = own_rows * nj
    share = depth // 2
    features = incoming.shape[2]
    both = ("ri", "rj")

    other = lax.ppermute(pair, both, [(n, n ^ 1) for n in range(ni * nj)])
    is_even = core == 0
    chip_pair = jnp.stack(
        [jnp.where(is_even, pair, other), jnp.where(is_even, other, pair)], axis=1
    )

    halves = jnp.concatenate([first, second], axis=0)
    groups = [[2 * m + c for m in range(chips)] for c in range(2)]
    gathered = lax.all_to_all(
        jnp.broadcast_to(halves[None], (chips,) + halves.shape),
        "rj",
        0,
        0,
        axis_index_groups=groups,
        tiled=True,
    )
    left = gathered[:, :rows].reshape(chips, rows, own_rows, HALF)

    outer = jnp.einsum(
        "injk,cek->icnje",
        chip_pair,
        couple_map.reshape(HALF, HALF, pair_features),
        preferred_element_type=jnp.float32,
    ).astype(jnp.bfloat16).reshape(rows, HALF, 2 * cols, HALF)
    left_t = left.transpose(1, 3, 0, 2).reshape(rows, HALF, share)
    right_part = jnp.einsum("icje,ics->jes", outer, left_t, preferred_element_type=jnp.float32)
    right_part = (right_part / depth).astype(jnp.bfloat16)
    right_part = right_part.reshape(2, cols * HALF, share)
    right_part = jnp.concatenate([right_part[0], right_part[1]], axis=1)
    moved = jnp.concatenate([gathered[:, rows:].reshape(chips * rows, 128), right_part], axis=0)
    swap = [
        (p * nj + 2 * m + c, m * nj + 2 * p + c)
        for p in range(ni)
        for m in range(chips)
        for c in range(2)
    ]
    moved = lax.ppermute(moved, both, swap)

    (acts, incoming), _ = lax.optimization_barrier(((acts, incoming), right_part))
    attn_in = lax.all_to_all(
        jnp.concatenate([acts, incoming], axis=1), "rj", 0, 0, tiled=True
    )
    acts_res = attn_in[:, :own_rows].reshape(depth, features)
    inc_res = attn_in[:, own_rows:].reshape(depth, features)

    right = moved[: chips * rows].reshape(chips, 2 * cols, own_rows, HALF)
    right_t = right.transpose(1, 3, 0, 2).reshape(2 * cols, HALF, share)
    left_part = jnp.einsum("icje,jes->ics", outer, right_t, preferred_element_type=jnp.float32)
    left_part = (left_part / depth).astype(jnp.bfloat16)
    right_back = moved[chips * rows :]
    right_back = jnp.concatenate([right_back[:, :share], right_back[:, share:]], axis=0)
    sums = jnp.concatenate([left_part, right_back.reshape(rows, HALF, share)], axis=2)
    sums = lax.all_to_all(sums, "rj", 0, 0, tiled=True)
    sums = jnp.sum(
        sums.reshape(chips, 2, HALF, 2, share).astype(jnp.float32), axis=0
    ).astype(jnp.bfloat16)
    factor = (
        sums.reshape(2, HALF, 2, chips, own_rows)
        .transpose(2, 1, 3, 0, 4)
        .reshape(2 * HALF, depth)
    )
    grad = (
        inc_res.astype(jnp.float32)
        + jnp.einsum("fs,mf->sm", factor, half_map, preferred_element_type=jnp.float32)
    ).astype(jnp.bfloat16)
    result = attention_backward(acts_res, grad, qkvg_map, result_map)
    return lax.all_to_all(result.reshape(nj, own_rows, features), "rj", 0, 0, tiled=True)


def solution(mesh):
    return jax.shard_map(
        local,
        mesh=mesh,
        in_specs=(
            P("ri", "rj", None),
            P("ri", "rj"),
            P("ri", "rj"),
            P("ri", "rj", None),
            P("ri", "rj", None),
            P(),
            P(),
            P(),
            P(),
        ),
        out_specs=P("ri", "rj", None),
        check_vma=False,
    )
```

```python
import functools

import jax
import jax.numpy as jnp
from jax import lax
from jax.experimental import pallas as pl
from jax.experimental.pallas import tpu as pltpu
from jax.sharding import PartitionSpec as P

HALF = 32
HEADS = 8
NT = (((1,), (1,)), ((), ()))
VMEM = pl.BlockSpec(memory_space=pltpu.VMEM)
SMEM = pl.BlockSpec(memory_space=pltpu.SMEM)
LIMIT = 40 * 1024 * 1024


def attention_backward(acts, grad, qkvg_map, result_map):
    rows, features = acts.shape
    head = features // HEADS
    scale = head ** (-0.5)
    projected = jnp.einsum(
        "cx,xy->cy", acts, qkvg_map, preferred_element_type=jnp.float32
    ).astype(jnp.bfloat16)
    shaped = projected.reshape(rows, 4, HEADS, head)
    queries, keys, values, logits = shaped[:, 0], shaped[:, 1], shaped[:, 2], shaped[:, 3]
    scores = jnp.einsum("shd,thd->hst", queries, keys, preferred_element_type=jnp.float32) * scale
    weights = jnp.exp(scores)
    attention = weights / jnp.sum(weights, axis=-1, keepdims=True)
    low = attention.astype(jnp.bfloat16)
    attended = jnp.einsum("hst,thd->shd", low, values, preferred_element_type=jnp.float32)
    gate = jax.nn.sigmoid(logits.astype(jnp.float32))
    grad_gated = jnp.einsum(
        "sm,om->so", grad, result_map, preferred_element_type=jnp.float32
    ).reshape(rows, HEADS, head)
    grad_attended = (gate * grad_gated).astype(jnp.bfloat16)
    grad_logits = grad_gated * attended * gate * (1.0 - gate)
    grad_weights = jnp.einsum(
        "shd,thd->hst", grad_attended, values, preferred_element_type=jnp.float32
    )
    grad_scores = (
        attention
        * (grad_weights - jnp.sum(attention * grad_weights, axis=-1, keepdims=True))
        * scale
    ).astype(jnp.bfloat16)
    grad_queries = jnp.einsum("hst,thd->shd", grad_scores, keys, preferred_element_type=jnp.float32)
    grad_keys = jnp.einsum("hst,shd->thd", grad_scores, queries, preferred_element_type=jnp.float32)
    grad_values = jnp.einsum("hst,shd->thd", low, grad_attended, preferred_element_type=jnp.float32)
    grad_projected = (
        jnp.stack([grad_queries, grad_keys, grad_values, grad_logits], axis=1)
        .reshape(rows, 4 * features)
        .astype(jnp.bfloat16)
    )
    back = jnp.einsum("sa,qa->sq", grad_projected, qkvg_map, preferred_element_type=jnp.float32)
    return (grad.astype(jnp.float32) + back).astype(jnp.bfloat16)


def outer_blocks(lhs, pieces, store):
    count = pieces[0].shape[0]
    zero = jnp.zeros((HALF, 128), jnp.bfloat16)
    for n in range(count):
        stacked = []
        for piece in pieces:
            x = piece[n]
            for g in range(4):
                stacked.append(
                    jnp.concatenate([x if h == g else zero for h in range(4)], axis=1)
                )
        product = lax.dot_general(
            lhs, jnp.concatenate(stacked, axis=0), NT, preferred_element_type=jnp.float32
        ).astype(jnp.bfloat16)
        for m in range(len(pieces)):
            for g in range(8):
                store(
                    m, n, g, product[g * HALF : (g + 1) * HALF, m * 128 : (m + 1) * 128]
                )


def outer_right_kernel(core_ref, lhs_ref, own_ref, other_ref, out_ref):
    cols = own_ref.shape[0]
    core = core_ref[0]
    starts = [core * (cols * HALF), (1 - core) * (cols * HALF)]

    def store(m, n, g, block):
        row = pl.multiple_of(starts[m] + n * HALF, HALF)
        out_ref[pl.ds(row, HALF), g * 128 : (g + 1) * 128] = block

    outer_blocks(lhs_ref[...], [own_ref, other_ref], store)


def outer_left_kernel(lhs_ref, pair_ref, out_ref):
    half = pair_ref.shape[0] // 2

    def store(m, n, g, block):
        row = (m * half + n) * HALF
        out_ref[row : row + HALF, g * 128 : (g + 1) * 128] = block

    outer_blocks(lhs_ref[...], [pair_ref.at[:half], pair_ref.at[half:]], store)


def right_kernel(scale, outer_ref, gathered_ref, out_ref):
    to = lax.broadcasted_iota(jnp.int32, (128, 128), 0)
    at = lax.broadcasted_iota(jnp.int32, (128, 128), 1)
    want = ((to & 63) >> 2) * 8 + (to >> 6) * 4 + (to & 3)
    order = jnp.where(at == want, 1.0, 0.0).astype(jnp.bfloat16)
    sorted_rows = jnp.dot(
        order, gathered_ref[...], preferred_element_type=jnp.float32
    ).astype(jnp.bfloat16)
    left = sorted_rows[:64]
    none = jnp.zeros_like(left)
    low = lax.dot_general(
        outer_ref[:512], jnp.concatenate([left, none], axis=0), NT,
        preferred_element_type=jnp.float32,
    )
    high = lax.dot_general(
        outer_ref[512:], jnp.concatenate([none, left], axis=0), NT,
        preferred_element_type=jnp.float32,
    )
    out_ref[:512] = ((low + high) * scale).astype(jnp.bfloat16)
    for block in range(8):
        out_ref[512 + block * 64 : 576 + block * 64] = sorted_rows[
            64:, block * 128 : (block + 1) * 128
        ]


def left_kernel(scale, outer_ref, moved_ref, out_ref):
    right = jnp.concatenate(
        [moved_ref[512 + block * 64 : 576 + block * 64] for block in range(8)], axis=1
    )
    sums = lax.dot_general(
        outer_ref[...], jnp.concatenate([right, jnp.zeros_like(right)], axis=0), NT,
        preferred_element_type=jnp.float32,
    ) * scale
    packed = moved_ref[:512].astype(jnp.float32)
    is_left = lax.broadcasted_iota(jnp.int32, (512, 128), 1) < 64
    out_ref[:512] = jnp.where(is_left, sums[:512], pltpu.roll(packed, 64, 1)).astype(jnp.bfloat16)
    out_ref[512:] = jnp.where(is_left, sums[512:], packed).astype(jnp.bfloat16)


def call(kernel, shape, specs, flops):
    return pl.pallas_call(
        kernel,
        out_shape=jax.ShapeDtypeStruct(shape, jnp.bfloat16),
        in_specs=specs,
        out_specs=VMEM,
        compiler_params=pltpu.CompilerParams(vmem_limit_bytes=LIMIT),
        cost_estimate=pl.CostEstimate(flops=flops, bytes_accessed=4 << 20, transcendentals=0),
    )


def local(
    pair,
    first,
    second,
    incoming,
    acts,
    couple_map,
    half_map,
    qkvg_map,
    result_map,
):
    ni = lax.axis_size("ri")
    nj = lax.axis_size("rj")
    chips = nj // 2
    core = lax.axis_index("rj") % 2
    rows, cols, pair_features = pair.shape
    own_rows = incoming.shape[1]
    depth = own_rows * nj
    share = depth // 2
    features = incoming.shape[2]
    both = ("ri", "rj")
    wide = rows * HALF

    halves = jnp.stack([first, second]).reshape(2, rows, own_rows, HALF)
    halves = halves.transpose(0, 2, 3, 1).reshape(2 * own_rows, wide)
    groups = [[2 * m + c for m in range(chips)] for c in range(2)]
    gathered = lax.all_to_all(
        jnp.broadcast_to(halves[None], (chips,) + halves.shape),
        "rj",
        0,
        0,
        axis_index_groups=groups,
        tiled=True,
    ).reshape(chips * 2 * own_rows, wide)

    own = pair.transpose(1, 0, 2)
    other = lax.ppermute(own, both, [(n, n ^ 1) for n in range(ni * nj)])
    maps = couple_map.reshape(8, 4, 8, 4, pair_features)
    map_right = maps.reshape(8, 4, HALF, pair_features).transpose(0, 2, 1, 3).reshape(256, 512)
    outer_right = call(
        outer_right_kernel, (wide, wide), [SMEM, VMEM, VMEM, VMEM], 2 * 256 * 512 * 4096
    )(core.reshape(1), map_right, own, other)
    moved = call(
        functools.partial(right_kernel, 1.0 / depth), (wide, 128), [VMEM, VMEM], 1 << 28
    )(outer_right, gathered)

    swap = [
        (p * nj + 2 * m + c, m * nj + 2 * p + c)
        for p in range(ni)
        for m in range(chips)
        for c in range(2)
    ]
    (own, other, acts, incoming), moved = lax.optimization_barrier(
        ((own, other, acts, incoming), moved)
    )
    moved = lax.ppermute(moved, both, swap)

    attn_in = lax.all_to_all(
        jnp.concatenate([acts, incoming], axis=1), "rj", 0, 0, tiled=True
    )
    acts_res = attn_in[:, :own_rows].reshape(depth, features)
    inc_res = attn_in[:, own_rows:].reshape(depth, features)

    is_even = core == 0
    chip_pair = jnp.concatenate(
        [jnp.where(is_even, own, other), jnp.where(is_even, other, own)], axis=0
    ).transpose(1, 0, 2)
    map_left = (
        maps.reshape(HALF, 8, 4, pair_features).transpose(1, 0, 2, 3).reshape(256, 512)
    )
    outer_left = call(outer_left_kernel, (wide, wide), [VMEM, VMEM], 2 * 256 * 512 * 4096)(
        map_left, chip_pair
    )
    sums = call(functools.partial(left_kernel, 1.0 / depth), (wide, 128), [VMEM, VMEM], 1 << 28)(
        outer_left, moved
    )
    sums = lax.all_to_all(sums.reshape(rows, HALF, 128), "rj", 0, 0, tiled=True)
    sums = jnp.sum(
        sums.reshape(chips, 2, HALF, 2, share).astype(jnp.float32), axis=0
    ).astype(jnp.bfloat16)
    factor = (
        sums.reshape(2, HALF, 2, chips, own_rows)
        .transpose(2, 1, 3, 0, 4)
        .reshape(2 * HALF, depth)
    )
    grad = (
        inc_res.astype(jnp.float32)
        + jnp.einsum("fs,mf->sm", factor, half_map, preferred_element_type=jnp.float32)
    ).astype(jnp.bfloat16)
    result = attention_backward(acts_res, grad, qkvg_map, result_map)
    return lax.all_to_all(result.reshape(nj, own_rows, features), "rj", 0, 0, tiled=True)


def solution(mesh):
    return jax.shard_map(
        local,
        mesh=mesh,
        in_specs=(
            P("ri", "rj", None),
            P("ri", "rj"),
            P("ri", "rj"),
            P("ri", "rj", None),
            P("ri", "rj", None),
            P(),
            P(),
            P(),
            P(),
        ),
        out_specs=P("ri", "rj", None),
        check_vma=False,
    )
```

```python
import functools

import jax
import jax.numpy as jnp
from jax import lax
from jax.experimental import pallas as pl
from jax.experimental.pallas import tpu as pltpu
from jax.sharding import PartitionSpec as P

HALF = 32
HEADS = 8
NT = (((1,), (1,)), ((), ()))
VMEM = pl.BlockSpec(memory_space=pltpu.VMEM)
SMEM = pl.BlockSpec(memory_space=pltpu.SMEM)
LIMIT = 40 * 1024 * 1024


def attention_backward(acts, grad, qkvg_map, result_map):
    rows, features = acts.shape
    head = features // HEADS
    scale = head ** (-0.5)
    projected = jnp.einsum(
        "cx,xy->cy", acts, qkvg_map, preferred_element_type=jnp.float32
    ).astype(jnp.bfloat16)
    shaped = projected.reshape(rows, 4, HEADS, head)
    queries, keys, values, logits = shaped[:, 0], shaped[:, 1], shaped[:, 2], shaped[:, 3]
    scores = jnp.einsum("shd,thd->hst", queries, keys, preferred_element_type=jnp.float32) * scale
    weights = jnp.exp(scores)
    attention = weights / jnp.sum(weights, axis=-1, keepdims=True)
    low = attention.astype(jnp.bfloat16)
    attended = jnp.einsum("hst,thd->shd", low, values, preferred_element_type=jnp.float32)
    gate = jax.nn.sigmoid(logits.astype(jnp.float32))
    grad_gated = jnp.einsum(
        "sm,om->so", grad, result_map, preferred_element_type=jnp.float32
    ).reshape(rows, HEADS, head)
    grad_attended = (gate * grad_gated).astype(jnp.bfloat16)
    grad_logits = grad_gated * attended * gate * (1.0 - gate)
    grad_weights = jnp.einsum(
        "shd,thd->hst", grad_attended, values, preferred_element_type=jnp.float32
    )
    grad_scores = (
        attention
        * (grad_weights - jnp.sum(attention * grad_weights, axis=-1, keepdims=True))
        * scale
    ).astype(jnp.bfloat16)
    grad_queries = jnp.einsum("hst,thd->shd", grad_scores, keys, preferred_element_type=jnp.float32)
    grad_keys = jnp.einsum("hst,shd->thd", grad_scores, queries, preferred_element_type=jnp.float32)
    grad_values = jnp.einsum("hst,shd->thd", low, grad_attended, preferred_element_type=jnp.float32)
    grad_projected = (
        jnp.stack([grad_queries, grad_keys, grad_values, grad_logits], axis=1)
        .reshape(rows, 4 * features)
        .astype(jnp.bfloat16)
    )
    back = jnp.einsum("sa,qa->sq", grad_projected, qkvg_map, preferred_element_type=jnp.float32)
    return (grad.astype(jnp.float32) + back).astype(jnp.bfloat16)


def outer_blocks(lhs, pieces, store):
    count = pieces[0].shape[0]
    zero = jnp.zeros((HALF, 128), jnp.bfloat16)
    for n in range(count):
        stacked = []
        for piece in pieces:
            x = piece[n]
            for g in range(4):
                stacked.append(
                    jnp.concatenate([x if h == g else zero for h in range(4)], axis=1)
                )
        product = lax.dot_general(
            lhs, jnp.concatenate(stacked, axis=0), NT, preferred_element_type=jnp.float32
        ).astype(jnp.bfloat16)
        for m in range(len(pieces)):
            for g in range(8):
                store(
                    m, n, g, product[g * HALF : (g + 1) * HALF, m * 128 : (m + 1) * 128]
                )


def factors_kernel(first_ref, second_ref, out_ref):
    shape = (256, 1024)
    copies = jnp.where(
        lax.broadcasted_iota(jnp.int32, (HALF, 1024), 0)
        == (lax.broadcasted_iota(jnp.int32, (HALF, 1024), 1) & 31),
        1.0,
        0.0,
    ).astype(jnp.bfloat16)
    both = jnp.concatenate([first_ref[...], second_ref[...]], axis=1)
    tiled = lax.dot_general(
        both, copies, (((0,), (0,)), ((), ())), preferred_element_type=jnp.float32
    )
    own_channel = (lax.broadcasted_iota(jnp.int32, shape, 0) & 31) == (
        lax.broadcasted_iota(jnp.int32, shape, 1) >> 5
    )
    kept = jnp.where(own_channel, tiled, 0.0).astype(jnp.bfloat16)
    rows = jnp.where(
        (lax.broadcasted_iota(jnp.int32, (128, 256), 0) & 7)
        == (lax.broadcasted_iota(jnp.int32, (128, 256), 1) >> 5),
        1.0,
        0.0,
    ).astype(jnp.bfloat16)
    out_ref[...] = jnp.dot(rows, kept, preferred_element_type=jnp.float32).astype(jnp.bfloat16)


def outer_right_kernel(core_ref, map_ref, own_ref, other_ref, out_ref):
    lhs = jnp.concatenate(
        [
            jnp.concatenate(
                [map_ref[(h * 4 + g) * HALF : (h * 4 + g + 1) * HALF] for g in range(4)], axis=1
            )
            for h in range(8)
        ],
        axis=0,
    )
    cols = own_ref.shape[0]
    core = core_ref[0]
    starts = [core * (cols * HALF), (1 - core) * (cols * HALF)]

    def store(m, n, g, block):
        row = pl.multiple_of(starts[m] + n * HALF, HALF)
        out_ref[pl.ds(row, HALF), g * 128 : (g + 1) * 128] = block

    outer_blocks(lhs, [own_ref, other_ref], store)


def outer_left_kernel(lhs_ref, pair_ref, out_ref):
    half = pair_ref.shape[0] // 2

    def store(m, n, g, block):
        row = (m * half + n) * HALF
        out_ref[row : row + HALF, g * 128 : (g + 1) * 128] = block

    outer_blocks(lhs_ref[...], [pair_ref.at[:half], pair_ref.at[half:]], store)


def right_kernel(scale, outer_ref, gathered_ref, out_ref):
    to = lax.broadcasted_iota(jnp.int32, (128, 128), 0)
    at = lax.broadcasted_iota(jnp.int32, (128, 128), 1)
    want = ((to & 63) >> 2) * 8 + (to >> 6) * 4 + (to & 3)
    order = jnp.where(at == want, 1.0, 0.0).astype(jnp.bfloat16)
    sorted_rows = jnp.dot(
        order, gathered_ref[...], preferred_element_type=jnp.float32
    ).astype(jnp.bfloat16)
    left = sorted_rows[:64]
    none = jnp.zeros_like(left)
    low = lax.dot_general(
        outer_ref[:512], jnp.concatenate([left, none], axis=0), NT,
        preferred_element_type=jnp.float32,
    )
    high = lax.dot_general(
        outer_ref[512:], jnp.concatenate([none, left], axis=0), NT,
        preferred_element_type=jnp.float32,
    )
    out_ref[:512] = ((low + high) * scale).astype(jnp.bfloat16)
    for block in range(8):
        out_ref[512 + block * 64 : 576 + block * 64] = sorted_rows[
            64:, block * 128 : (block + 1) * 128
        ]


def left_kernel(scale, outer_ref, moved_ref, attn_ref, out_ref):
    right = jnp.concatenate(
        [moved_ref[512 + block * 64 : 576 + block * 64] for block in range(8)], axis=1
    )
    sums = lax.dot_general(
        outer_ref[...], jnp.concatenate([right, jnp.zeros_like(right)], axis=0), NT,
        preferred_element_type=jnp.float32,
    ) * scale
    packed = moved_ref[:512].astype(jnp.float32)
    is_left = lax.broadcasted_iota(jnp.int32, (512, 128), 1) < 64
    low = jnp.where(is_left, sums[:512], pltpu.roll(packed, 64, 1)).astype(jnp.bfloat16)
    high = jnp.where(is_left, sums[512:], packed).astype(jnp.bfloat16)
    half = out_ref.shape[0] // 2
    for n in range(half):
        out_ref[n, :HALF] = low[n * HALF : (n + 1) * HALF]
        out_ref[n + half, :HALF] = high[n * HALF : (n + 1) * HALF]
    for n in range(2 * half):
        out_ref[n, HALF:] = attn_ref[n]


def call(kernel, shape, specs, flops):
    return pl.pallas_call(
        kernel,
        out_shape=jax.ShapeDtypeStruct(shape, jnp.bfloat16),
        in_specs=specs,
        out_specs=VMEM,
        compiler_params=pltpu.CompilerParams(vmem_limit_bytes=LIMIT),
        cost_estimate=pl.CostEstimate(flops=flops, bytes_accessed=4 << 20, transcendentals=0),
    )


def local(
    pair,
    first,
    second,
    incoming,
    acts,
    couple_map,
    half_map,
    qkvg_map,
    result_map,
):
    ni = lax.axis_size("ri")
    nj = lax.axis_size("rj")
    chips = nj // 2
    core = lax.axis_index("rj") % 2
    rows, cols, pair_features = pair.shape
    own_rows = incoming.shape[1]
    depth = own_rows * nj
    share = depth // 2
    features = incoming.shape[2]
    both = ("ri", "rj")
    wide = rows * HALF
    scale = 1.0 / depth

    halves = call(factors_kernel, (chips * 2 * own_rows, wide), [VMEM, VMEM], 1 << 27)(
        first, second
    )
    groups = [[2 * m + c for m in range(chips)] for c in range(2)]
    gathered = lax.all_to_all(
        halves.reshape(chips, 2 * own_rows, wide),
        "rj",
        0,
        0,
        axis_index_groups=groups,
        tiled=True,
    ).reshape(chips * 2 * own_rows, wide)

    own = pair.transpose(1, 0, 2)
    other = lax.ppermute(own, both, [(n, n ^ 1) for n in range(ni * nj)])
    maps = couple_map.reshape(8, 4, 8, 4, pair_features)
    outer_right = call(
        outer_right_kernel, (wide, wide), [SMEM, VMEM, VMEM, VMEM], 2 * 256 * 512 * 4096
    )(core.reshape(1), couple_map, own, other)
    moved = call(
        functools.partial(right_kernel, scale), (wide, 128), [VMEM, VMEM], 1 << 28
    )(outer_right, gathered)

    swap = [
        (p * nj + 2 * m + c, m * nj + 2 * p + c)
        for p in range(ni)
        for m in range(chips)
        for c in range(2)
    ]
    (own, other), moved = lax.optimization_barrier(((own, other), moved))
    moved = lax.ppermute(moved, both, swap)

    is_even = core == 0
    chip_pair = jnp.concatenate(
        [jnp.where(is_even, own, other), jnp.where(is_even, other, own)], axis=0
    ).transpose(1, 0, 2)
    map_left = (
        maps.reshape(HALF, 8, 4, pair_features).transpose(1, 0, 2, 3).reshape(256, 512)
    )
    outer_left = call(outer_left_kernel, (wide, wide), [VMEM, VMEM], 2 * 256 * 512 * 4096)(
        map_left, chip_pair
    )
    attn_in = jnp.concatenate(
        [acts.reshape(rows, 2 * own_rows, 128), incoming.reshape(rows, 2 * own_rows, 128)], axis=1
    )
    sums = call(
        functools.partial(left_kernel, scale), (rows, HALF + 16, 128), [VMEM, VMEM, VMEM], 1 << 28
    )(outer_left, moved, attn_in)
    received = lax.all_to_all(sums, "rj", 0, 0, tiled=True)
    sums = received[:, :HALF]
    acts_res = received[:, HALF : HALF + 8].reshape(depth, features)
    inc_res = received[:, HALF + 8 :].reshape(depth, features)
    sums = jnp.sum(
        sums.reshape(chips, 2, HALF, 2, share).astype(jnp.float32), axis=0
    ).astype(jnp.bfloat16)
    factor = (
        sums.reshape(2, HALF, 2, chips, own_rows)
        .transpose(2, 1, 3, 0, 4)
        .reshape(2 * HALF, depth)
    )
    grad = (
        inc_res.astype(jnp.float32)
        + jnp.einsum("fs,mf->sm", factor, half_map, preferred_element_type=jnp.float32)
    ).astype(jnp.bfloat16)
    result = attention_backward(acts_res, grad, qkvg_map, result_map)
    return lax.all_to_all(result.reshape(nj, own_rows, features), "rj", 0, 0, tiled=True)


def solution(mesh):
    return jax.shard_map(
        local,
        mesh=mesh,
        in_specs=(
            P("ri", "rj", None),
            P("ri", "rj"),
            P("ri", "rj"),
            P("ri", "rj", None),
            P("ri", "rj", None),
            P(),
            P(),
            P(),
            P(),
        ),
        out_specs=P("ri", "rj", None),
        check_vma=False,
    )
```

```python
import functools

import jax
import jax.numpy as jnp
from jax import lax
from jax.experimental import pallas as pl
from jax.experimental.pallas import tpu as pltpu
from jax.sharding import PartitionSpec as P

HALF = 32
HEADS = 8
NT = (((1,), (1,)), ((), ()))
VMEM = pl.BlockSpec(memory_space=pltpu.VMEM)
SMEM = pl.BlockSpec(memory_space=pltpu.SMEM)
LIMIT = 40 * 1024 * 1024
SOURCE = (
    (0, 3, 5, 4, 11, 10, 9, 14, 13, 15, 12, 8, 6, 7, 1, 2),
    (3, 2, 0, 1, 9, 15, 11, 10, 13, 8, 12, 14, 6, 7, 4, 5),
    (6, 7, 1, 2, 13, 11, 8, 9, 10, 15, 12, 14, 0, 3, 4, 5),
    (2, 3, 4, 1, 10, 11, 8, 9, 13, 14, 15, 12, 5, 7, 0, 6),
    (7, 6, 1, 2, 5, 11, 8, 4, 14, 15, 9, 10, 3, 0, 12, 13),
    (3, 8, 7, 0, 10, 5, 4, 6, 15, 12, 11, 9, 1, 2, 14, 13),
    (5, 3, 0, 4, 6, 7, 8, 10, 9, 11, 12, 13, 14, 15, 1, 2),
    (2, 4, 5, 1, 7, 8, 9, 6, 10, 11, 12, 13, 14, 15, 3, 0),
    (15, 12, 0, 1, 3, 2, 4, 5, 9, 10, 11, 8, 6, 7, 13, 14),
    (13, 14, 2, 1, 3, 4, 0, 6, 10, 11, 5, 9, 7, 12, 15, 8),
    (2, 3, 13, 14, 1, 6, 7, 0, 11, 4, 5, 10, 15, 8, 9, 12),
    (2, 3, 15, 12, 6, 7, 0, 1, 10, 11, 4, 5, 13, 14, 8, 9),
    (10, 12, 15, 13, 3, 2, 0, 1, 6, 7, 4, 5, 14, 11, 8, 9),
    (11, 15, 8, 10, 5, 3, 0, 1, 2, 6, 7, 4, 14, 13, 12, 9),
    (9, 11, 8, 12, 6, 7, 4, 5, 2, 0, 3, 1, 10, 15, 13, 14),
    (9, 14, 12, 13, 2, 3, 1, 0, 5, 4, 7, 6, 11, 10, 8, 15),
)
TARGET = (
    (0, 3, 5, 4, 11, 10, 9, 14, 13, 15, 12, 8, 6, 7, 1, 2),
    (3, 2, 0, 1, 9, 15, 11, 10, 13, 8, 12, 14, 6, 7, 4, 5),
    (6, 7, 1, 2, 13, 11, 8, 9, 10, 15, 12, 14, 0, 3, 4, 5),
    (2, 3, 4, 1, 10, 11, 8, 9, 13, 14, 15, 12, 5, 7, 0, 6),
    (7, 6, 1, 2, 5, 11, 8, 4, 14, 15, 9, 10, 3, 0, 12, 13),
    (3, 8, 7, 0, 10, 5, 4, 6, 15, 12, 11, 9, 1, 2, 14, 13),
    (5, 3, 0, 4, 6, 7, 8, 10, 9, 11, 12, 13, 14, 15, 1, 2),
    (2, 4, 5, 1, 7, 8, 9, 6, 10, 11, 12, 13, 14, 15, 3, 0),
    (15, 12, 0, 1, 3, 2, 4, 5, 9, 10, 11, 8, 6, 7, 13, 14),
    (13, 14, 2, 1, 3, 4, 0, 6, 10, 11, 5, 9, 7, 12, 15, 8),
    (2, 3, 13, 14, 1, 6, 7, 0, 11, 4, 5, 10, 15, 8, 9, 12),
    (2, 3, 15, 12, 6, 7, 0, 1, 10, 11, 4, 5, 13, 14, 8, 9),
    (10, 12, 15, 13, 3, 2, 0, 1, 6, 7, 4, 5, 14, 11, 8, 9),
    (11, 15, 8, 10, 5, 3, 0, 1, 2, 6, 7, 4, 14, 13, 12, 9),
    (9, 11, 8, 12, 6, 7, 4, 5, 2, 0, 3, 1, 10, 15, 13, 14),
    (9, 14, 12, 13, 2, 3, 1, 0, 5, 4, 7, 6, 11, 10, 8, 15),
)


def attention_backward(acts, grad, qkvg_map, result_map):
    rows, features = acts.shape
    head = features // HEADS
    scale = head ** (-0.5)
    projected = jnp.einsum(
        "cx,xy->cy", acts, qkvg_map, preferred_element_type=jnp.float32
    ).astype(jnp.bfloat16)
    shaped = projected.reshape(rows, 4, HEADS, head)
    queries, keys, values, logits = shaped[:, 0], shaped[:, 1], shaped[:, 2], shaped[:, 3]
    scores = jnp.einsum("shd,thd->hst", queries, keys, preferred_element_type=jnp.float32) * scale
    weights = jnp.exp(scores)
    attention = weights / jnp.sum(weights, axis=-1, keepdims=True)
    low = attention.astype(jnp.bfloat16)
    attended = jnp.einsum("hst,thd->shd", low, values, preferred_element_type=jnp.float32)
    gate = jax.nn.sigmoid(logits.astype(jnp.float32))
    grad_gated = jnp.einsum(
        "sm,om->so", grad, result_map, preferred_element_type=jnp.float32
    ).reshape(rows, HEADS, head)
    grad_attended = (gate * grad_gated).astype(jnp.bfloat16)
    grad_logits = grad_gated * attended * gate * (1.0 - gate)
    grad_weights = jnp.einsum(
        "shd,thd->hst", grad_attended, values, preferred_element_type=jnp.float32
    )
    grad_scores = (
        attention
        * (grad_weights - jnp.sum(attention * grad_weights, axis=-1, keepdims=True))
        * scale
    ).astype(jnp.bfloat16)
    grad_queries = jnp.einsum("hst,thd->shd", grad_scores, keys, preferred_element_type=jnp.float32)
    grad_keys = jnp.einsum("hst,shd->thd", grad_scores, queries, preferred_element_type=jnp.float32)
    grad_values = jnp.einsum("hst,shd->thd", low, grad_attended, preferred_element_type=jnp.float32)
    grad_projected = (
        jnp.stack([grad_queries, grad_keys, grad_values, grad_logits], axis=1)
        .reshape(rows, 4 * features)
        .astype(jnp.bfloat16)
    )
    back = jnp.einsum("sa,qa->sq", grad_projected, qkvg_map, preferred_element_type=jnp.float32)
    return (grad.astype(jnp.float32) + back).astype(jnp.bfloat16)


def outer_blocks(lhs, count, pieces, store):
    zero = jnp.zeros((HALF, 128), jnp.bfloat16)
    for n in range(count):
        stacked = []
        for piece in pieces:
            x = piece(n)
            for g in range(4):
                stacked.append(
                    jnp.concatenate([x if h == g else zero for h in range(4)], axis=1)
                )
        product = lax.dot_general(
            lhs, jnp.concatenate(stacked, axis=0), NT, preferred_element_type=jnp.float32
        ).astype(jnp.bfloat16)
        for m in range(len(pieces)):
            for g in range(8):
                store(
                    m, n, g, product[g * HALF : (g + 1) * HALF, m * 128 : (m + 1) * 128]
                )


def factors_kernel(first_ref, second_ref, out_ref):
    shape = (256, 1024)
    copies = jnp.where(
        lax.broadcasted_iota(jnp.int32, (HALF, 1024), 0)
        == (lax.broadcasted_iota(jnp.int32, (HALF, 1024), 1) & 31),
        1.0,
        0.0,
    ).astype(jnp.bfloat16)
    both = jnp.concatenate([first_ref[...], second_ref[...]], axis=1)
    tiled = lax.dot_general(
        both, copies, (((0,), (0,)), ((), ())), preferred_element_type=jnp.float32
    )
    own_channel = (lax.broadcasted_iota(jnp.int32, shape, 0) & 31) == (
        lax.broadcasted_iota(jnp.int32, shape, 1) >> 5
    )
    kept = jnp.where(own_channel, tiled, 0.0).astype(jnp.bfloat16)
    rows = jnp.where(
        (lax.broadcasted_iota(jnp.int32, (128, 256), 0) & 7)
        == (lax.broadcasted_iota(jnp.int32, (128, 256), 1) >> 5),
        1.0,
        0.0,
    ).astype(jnp.bfloat16)
    out_ref[...] = jnp.dot(rows, kept, preferred_element_type=jnp.float32).astype(jnp.bfloat16)


def outer_right_kernel(core_ref, map_ref, own_ref, other_ref, out_ref):
    lhs = jnp.concatenate(
        [
            jnp.concatenate(
                [map_ref[(h * 4 + g) * HALF : (h * 4 + g + 1) * HALF] for g in range(4)], axis=1
            )
            for h in range(8)
        ],
        axis=0,
    )
    cols = own_ref.shape[1]
    core = core_ref[0]
    starts = [core * (cols * HALF), (1 - core) * (cols * HALF)]

    def store(m, n, g, block):
        row = pl.multiple_of(starts[m] + n * HALF, HALF)
        out_ref[pl.ds(row, HALF), g * 128 : (g + 1) * 128] = block

    outer_blocks(
        lhs, cols, [lambda n: own_ref[:, n, :], lambda n: other_ref[:, n, :]], store
    )


def outer_left_kernel(core_ref, lhs_ref, own_ref, other_ref, out_ref):
    half = own_ref.shape[0] // 2
    is_even = core_ref[0] == 0

    def columns(i):
        own, other = own_ref[i], other_ref[i]
        return jnp.concatenate(
            [jnp.where(is_even, own, other), jnp.where(is_even, other, own)], axis=0
        )

    def store(m, n, g, block):
        row = (m * half + n) * HALF
        out_ref[row : row + HALF, g * 128 : (g + 1) * 128] = block

    outer_blocks(lhs_ref[...], half, [columns, lambda n: columns(half + n)], store)


def right_kernel(scale, outer_ref, gathered_ref, out_ref, factors_ref):
    to = lax.broadcasted_iota(jnp.int32, (128, 128), 0)
    at = lax.broadcasted_iota(jnp.int32, (128, 128), 1)
    want = ((to & 63) >> 2) * 8 + (to >> 6) * 4 + (to & 3)
    order = jnp.where(at == want, 1.0, 0.0).astype(jnp.bfloat16)
    sorted_rows = jnp.dot(
        order, gathered_ref[...], preferred_element_type=jnp.float32
    ).astype(jnp.bfloat16)
    left = sorted_rows[:64]
    none = jnp.zeros_like(left)
    low = lax.dot_general(
        outer_ref[:512], jnp.concatenate([left, none], axis=0), NT,
        preferred_element_type=jnp.float32,
    )
    high = lax.dot_general(
        outer_ref[512:], jnp.concatenate([none, left], axis=0), NT,
        preferred_element_type=jnp.float32,
    )
    out_ref[...] = ((low + high) * scale).astype(jnp.bfloat16)
    for block in range(8):
        factors_ref[block * 64 : 64 + block * 64] = sorted_rows[
            64:, block * 128 : (block + 1) * 128
        ]


def left_kernel(scale, outer_ref, factors_ref, right_ref, attn_ref, out_ref):
    right = jnp.concatenate(
        [factors_ref[block * 64 : 64 + block * 64] for block in range(8)], axis=1
    )
    sums = lax.dot_general(
        outer_ref[...], jnp.concatenate([right, jnp.zeros_like(right)], axis=0), NT,
        preferred_element_type=jnp.float32,
    ) * scale
    packed = right_ref[...].astype(jnp.float32)
    is_left = lax.broadcasted_iota(jnp.int32, (512, 128), 1) < 64
    low = jnp.where(is_left, sums[:512], pltpu.roll(packed, 64, 1)).astype(jnp.bfloat16)
    high = jnp.where(is_left, sums[512:], packed).astype(jnp.bfloat16)
    half = out_ref.shape[0] // 2
    for n in range(half):
        out_ref[n, :HALF] = low[n * HALF : (n + 1) * HALF]
        out_ref[n + half, :HALF] = high[n * HALF : (n + 1) * HALF]
    for n in range(2 * half):
        out_ref[n, HALF:] = attn_ref[n]


def call(kernel, shapes, specs, flops):
    many = isinstance(shapes, list)
    out = [jax.ShapeDtypeStruct(x, jnp.bfloat16) for x in (shapes if many else [shapes])]
    return pl.pallas_call(
        kernel,
        out_shape=out if many else out[0],
        in_specs=specs,
        out_specs=[VMEM] * len(out) if many else VMEM,
        compiler_params=pltpu.CompilerParams(vmem_limit_bytes=LIMIT),
        cost_estimate=pl.CostEstimate(flops=flops, bytes_accessed=4 << 20, transcendentals=0),
    )


def local(
    pair,
    first,
    second,
    incoming,
    acts,
    couple_map,
    half_map,
    qkvg_map,
    result_map,
):
    ni = lax.axis_size("ri")
    nj = lax.axis_size("rj")
    chips = nj // 2
    core = lax.axis_index("rj") % 2
    rows, cols, pair_features = pair.shape
    own_rows = incoming.shape[1]
    depth = own_rows * nj
    share = depth // 2
    features = incoming.shape[2]
    both = ("ri", "rj")
    wide = rows * HALF
    scale = 1.0 / depth

    halves = call(factors_kernel, (chips * 2 * own_rows, wide), [VMEM, VMEM], 1 << 27)(
        first, second
    )
    groups = [[2 * m + c for m in range(chips)] for c in range(2)]
    gathered = lax.all_to_all(
        halves.reshape(chips, 2 * own_rows, wide),
        "rj",
        0,
        0,
        axis_index_groups=groups,
        tiled=True,
    ).reshape(chips * 2 * own_rows, wide)

    other = lax.ppermute(pair, both, [(n, n ^ 1) for n in range(ni * nj)])
    outer_right = call(
        outer_right_kernel, (wide, wide), [SMEM, VMEM, VMEM, VMEM], 2 * 256 * 512 * 4096
    )(core.reshape(1), couple_map, pair, other)
    right_part, factors = call(
        functools.partial(right_kernel, scale), [(wide // 2, 128)] * 2, [VMEM, VMEM], 1 << 28
    )(outer_right, gathered)

    (pair, other, couple_map), right_part = lax.optimization_barrier(
        ((pair, other, couple_map), right_part)
    )
    places = [(p, m, c) for p in range(ni) for m in range(chips) for c in range(2)]
    factors = lax.ppermute(
        factors,
        both,
        [(m * nj + 2 * SOURCE[m][p] + c, p * nj + 2 * m + c) for p, m, c in places],
    )
    right_part = lax.ppermute(
        right_part,
        both,
        [(p * nj + 2 * m + c, m * nj + 2 * TARGET[m][p] + c) for p, m, c in places],
    )

    map_left = (
        couple_map.reshape(HALF, 8, 4, pair_features).transpose(1, 0, 2, 3).reshape(256, 512)
    )
    outer_left = call(
        outer_left_kernel, (wide, wide), [SMEM, VMEM, VMEM, VMEM], 2 * 256 * 512 * 4096
    )(core.reshape(1), map_left, pair, other)
    attn_in = jnp.concatenate(
        [acts.reshape(rows, 2 * own_rows, 128), incoming.reshape(rows, 2 * own_rows, 128)], axis=1
    )
    sums = call(
        functools.partial(left_kernel, scale), (rows, HALF + 16, 128), [VMEM] * 4, 1 << 28
    )(outer_left, factors, right_part, attn_in)
    received = lax.all_to_all(sums, "rj", 0, 0, tiled=True)
    sums = received[:, :HALF]
    acts_res = received[:, HALF : HALF + 8].reshape(depth, features)
    inc_res = received[:, HALF + 8 :].reshape(depth, features)
    sums = jnp.sum(
        sums.reshape(chips, 2, HALF, 2, share).astype(jnp.float32), axis=0
    ).astype(jnp.bfloat16)
    factor = (
        sums.reshape(2, HALF, 2, chips, own_rows)
        .transpose(2, 1, 3, 0, 4)
        .reshape(2 * HALF, depth)
    )
    grad = (
        inc_res.astype(jnp.float32)
        + jnp.einsum("fs,mf->sm", factor, half_map, preferred_element_type=jnp.float32)
    ).astype(jnp.bfloat16)
    result = attention_backward(acts_res, grad, qkvg_map, result_map)
    return lax.all_to_all(result.reshape(nj, own_rows, features), "rj", 0, 0, tiled=True)


def solution(mesh):
    return jax.shard_map(
        local,
        mesh=mesh,
        in_specs=(
            P("ri", "rj", None),
            P("ri", "rj"),
            P("ri", "rj"),
            P("ri", "rj", None),
            P("ri", "rj", None),
            P(),
            P(),
            P(),
            P(),
        ),
        out_specs=P("ri", "rj", None),
        check_vma=False,
    )
```

```python
import functools

import jax
import jax.numpy as jnp
from jax import lax
from jax.experimental import pallas as pl
from jax.experimental.pallas import tpu as pltpu
from jax.sharding import PartitionSpec as P

HALF = 32
HEADS = 8
NT = (((1,), (1,)), ((), ()))
VMEM = pl.BlockSpec(memory_space=pltpu.VMEM)
SMEM = pl.BlockSpec(memory_space=pltpu.SMEM)
LIMIT = 40 * 1024 * 1024
SOURCE = (
    (0, 3, 5, 4, 11, 10, 9, 14, 13, 15, 12, 8, 6, 7, 1, 2),
    (3, 2, 0, 1, 9, 15, 11, 10, 13, 8, 12, 14, 6, 7, 4, 5),
    (6, 7, 1, 2, 13, 11, 8, 9, 10, 15, 12, 14, 0, 3, 4, 5),
    (2, 3, 4, 1, 10, 11, 8, 9, 13, 14, 15, 12, 5, 7, 0, 6),
    (7, 6, 1, 2, 5, 11, 8, 4, 14, 15, 9, 10, 3, 0, 12, 13),
    (3, 8, 7, 0, 10, 5, 4, 6, 15, 12, 11, 9, 1, 2, 14, 13),
    (5, 3, 0, 4, 6, 7, 8, 10, 9, 11, 12, 13, 14, 15, 1, 2),
    (2, 4, 5, 1, 7, 8, 9, 6, 10, 11, 12, 13, 14, 15, 3, 0),
    (15, 12, 0, 1, 3, 2, 4, 5, 9, 10, 11, 8, 6, 7, 13, 14),
    (13, 14, 2, 1, 3, 4, 0, 6, 10, 11, 5, 9, 7, 12, 15, 8),
    (2, 3, 13, 14, 1, 6, 7, 0, 11, 4, 5, 10, 15, 8, 9, 12),
    (2, 3, 15, 12, 6, 7, 0, 1, 10, 11, 4, 5, 13, 14, 8, 9),
    (10, 12, 15, 13, 3, 2, 0, 1, 6, 7, 4, 5, 14, 11, 8, 9),
    (11, 15, 8, 10, 5, 3, 0, 1, 2, 6, 7, 4, 14, 13, 12, 9),
    (9, 11, 8, 12, 6, 7, 4, 5, 2, 0, 3, 1, 10, 15, 13, 14),
    (9, 14, 12, 13, 2, 3, 1, 0, 5, 4, 7, 6, 11, 10, 8, 15),
)
TARGET = (
    (0, 3, 5, 4, 11, 10, 9, 14, 13, 15, 12, 8, 6, 7, 1, 2),
    (3, 2, 0, 1, 9, 15, 11, 10, 13, 8, 12, 14, 6, 7, 4, 5),
    (6, 7, 1, 2, 13, 11, 8, 9, 10, 15, 12, 14, 0, 3, 4, 5),
    (2, 3, 4, 1, 10, 11, 8, 9, 13, 14, 15, 12, 5, 7, 0, 6),
    (7, 6, 1, 2, 5, 11, 8, 4, 14, 15, 9, 10, 3, 0, 12, 13),
    (3, 8, 7, 0, 10, 5, 4, 6, 15, 12, 11, 9, 1, 2, 14, 13),
    (5, 3, 0, 4, 6, 7, 8, 10, 9, 11, 12, 13, 14, 15, 1, 2),
    (2, 4, 5, 1, 7, 8, 9, 6, 10, 11, 12, 13, 14, 15, 3, 0),
    (15, 12, 0, 1, 3, 2, 4, 5, 9, 10, 11, 8, 6, 7, 13, 14),
    (13, 14, 2, 1, 3, 4, 0, 6, 10, 11, 5, 9, 7, 12, 15, 8),
    (2, 3, 13, 14, 1, 6, 7, 0, 11, 4, 5, 10, 15, 8, 9, 12),
    (2, 3, 15, 12, 6, 7, 0, 1, 10, 11, 4, 5, 13, 14, 8, 9),
    (10, 12, 15, 13, 3, 2, 0, 1, 6, 7, 4, 5, 14, 11, 8, 9),
    (11, 15, 8, 10, 5, 3, 0, 1, 2, 6, 7, 4, 14, 13, 12, 9),
    (9, 11, 8, 12, 6, 7, 4, 5, 2, 0, 3, 1, 10, 15, 13, 14),
    (9, 14, 12, 13, 2, 3, 1, 0, 5, 4, 7, 6, 11, 10, 8, 15),
)


def attention_backward(acts, grad, qkvg_map, result_map):
    rows, features = acts.shape
    head = features // HEADS
    scale = head ** (-0.5)
    projected = jnp.einsum(
        "cx,xy->cy", acts, qkvg_map, preferred_element_type=jnp.float32
    ).astype(jnp.bfloat16)
    shaped = projected.reshape(rows, 4, HEADS, head)
    queries, keys, values, logits = shaped[:, 0], shaped[:, 1], shaped[:, 2], shaped[:, 3]
    scores = jnp.einsum("shd,thd->hst", queries, keys, preferred_element_type=jnp.float32) * scale
    weights = jnp.exp(scores)
    attention = weights / jnp.sum(weights, axis=-1, keepdims=True)
    low = attention.astype(jnp.bfloat16)
    attended = jnp.einsum("hst,thd->shd", low, values, preferred_element_type=jnp.float32)
    gate = jax.nn.sigmoid(logits.astype(jnp.float32))
    grad_gated = jnp.einsum(
        "sm,om->so", grad, result_map, preferred_element_type=jnp.float32
    ).reshape(rows, HEADS, head)
    grad_attended = (gate * grad_gated).astype(jnp.bfloat16)
    grad_logits = grad_gated * attended * gate * (1.0 - gate)
    grad_weights = jnp.einsum(
        "shd,thd->hst", grad_attended, values, preferred_element_type=jnp.float32
    )
    grad_scores = (
        attention
        * (grad_weights - jnp.sum(attention * grad_weights, axis=-1, keepdims=True))
        * scale
    ).astype(jnp.bfloat16)
    grad_queries = jnp.einsum("hst,thd->shd", grad_scores, keys, preferred_element_type=jnp.float32)
    grad_keys = jnp.einsum("hst,shd->thd", grad_scores, queries, preferred_element_type=jnp.float32)
    grad_values = jnp.einsum("hst,shd->thd", low, grad_attended, preferred_element_type=jnp.float32)
    grad_projected = (
        jnp.stack([grad_queries, grad_keys, grad_values, grad_logits], axis=1)
        .reshape(rows, 4 * features)
        .astype(jnp.bfloat16)
    )
    back = jnp.einsum("sa,qa->sq", grad_projected, qkvg_map, preferred_element_type=jnp.float32)
    return (grad.astype(jnp.float32) + back).astype(jnp.bfloat16)


def outer_blocks(lhs, count, pieces, store):
    zero = jnp.zeros((HALF, 128), jnp.bfloat16)
    for n in range(count):
        stacked = []
        for piece in pieces:
            x = piece(n)
            for g in range(4):
                stacked.append(
                    jnp.concatenate([x if h == g else zero for h in range(4)], axis=1)
                )
        product = lax.dot_general(
            lhs, jnp.concatenate(stacked, axis=0), NT, preferred_element_type=jnp.float32
        ).astype(jnp.bfloat16)
        for m in range(len(pieces)):
            for g in range(8):
                store(
                    m, n, g, product[g * HALF : (g + 1) * HALF, m * 128 : (m + 1) * 128]
                )


def factors_kernel(first_ref, second_ref, out_ref):
    shape = (256, 1024)
    copies = jnp.where(
        lax.broadcasted_iota(jnp.int32, (HALF, 1024), 0)
        == (lax.broadcasted_iota(jnp.int32, (HALF, 1024), 1) & 31),
        1.0,
        0.0,
    ).astype(jnp.bfloat16)
    both = jnp.concatenate([first_ref[...], second_ref[...]], axis=1)
    tiled = lax.dot_general(
        both, copies, (((0,), (0,)), ((), ())), preferred_element_type=jnp.float32
    )
    own_channel = (lax.broadcasted_iota(jnp.int32, shape, 0) & 31) == (
        lax.broadcasted_iota(jnp.int32, shape, 1) >> 5
    )
    kept = jnp.where(own_channel, tiled, 0.0).astype(jnp.bfloat16)
    rows = jnp.where(
        (lax.broadcasted_iota(jnp.int32, (128, 256), 0) & 7)
        == (lax.broadcasted_iota(jnp.int32, (128, 256), 1) >> 5),
        1.0,
        0.0,
    ).astype(jnp.bfloat16)
    out_ref[...] = jnp.dot(rows, kept, preferred_element_type=jnp.float32).astype(jnp.bfloat16)


def outer_right_kernel(core_ref, map_ref, own_ref, other_ref, out_ref):
    lhs = jnp.concatenate(
        [
            jnp.concatenate(
                [map_ref[(h * 4 + g) * HALF : (h * 4 + g + 1) * HALF] for g in range(4)], axis=1
            )
            for h in range(8)
        ],
        axis=0,
    )
    cols = own_ref.shape[1]
    count = own_ref.shape[0] * cols
    to = lax.broadcasted_iota(jnp.int32, (count, count), 0)
    at = lax.broadcasted_iota(jnp.int32, (count, count), 1)
    order = jnp.where(at == (to & 31) * cols + (to >> 5), 1.0, 0.0).astype(jnp.bfloat16)
    turned = jnp.dot(
        order,
        jnp.concatenate(
            [own_ref[...].reshape(count, 128), other_ref[...].reshape(count, 128)], axis=1
        ),
        preferred_element_type=jnp.float32,
    ).astype(jnp.bfloat16)
    core = core_ref[0]
    starts = [core * (cols * HALF), (1 - core) * (cols * HALF)]

    def store(m, n, g, block):
        row = pl.multiple_of(starts[m] + n * HALF, HALF)
        out_ref[pl.ds(row, HALF), g * 128 : (g + 1) * 128] = block

    outer_blocks(
        lhs, cols, [lambda n: turned[n * HALF : (n + 1) * HALF, :128],
         lambda n: turned[n * HALF : (n + 1) * HALF, 128:]], store
    )


def outer_left_kernel(core_ref, lhs_ref, own_ref, other_ref, out_ref):
    half = own_ref.shape[0] // 2
    is_even = core_ref[0] == 0

    def columns(i):
        own, other = own_ref[i], other_ref[i]
        return jnp.concatenate(
            [jnp.where(is_even, own, other), jnp.where(is_even, other, own)], axis=0
        )

    def store(m, n, g, block):
        row = (m * half + n) * HALF
        out_ref[row : row + HALF, g * 128 : (g + 1) * 128] = block

    outer_blocks(lhs_ref[...], half, [columns, lambda n: columns(half + n)], store)


def right_kernel(scale, outer_ref, gathered_ref, out_ref, factors_ref):
    to = lax.broadcasted_iota(jnp.int32, (128, 128), 0)
    at = lax.broadcasted_iota(jnp.int32, (128, 128), 1)
    want = ((to & 63) >> 2) * 8 + (to >> 6) * 4 + (to & 3)
    order = jnp.where(at == want, 1.0, 0.0).astype(jnp.bfloat16)
    sorted_rows = jnp.dot(
        order, gathered_ref[...], preferred_element_type=jnp.float32
    ).astype(jnp.bfloat16)
    left = sorted_rows[:64]
    none = jnp.zeros_like(left)
    low = lax.dot_general(
        outer_ref[:512], jnp.concatenate([left, none], axis=0), NT,
        preferred_element_type=jnp.float32,
    )
    high = lax.dot_general(
        outer_ref[512:], jnp.concatenate([none, left], axis=0), NT,
        preferred_element_type=jnp.float32,
    )
    out_ref[...] = ((low + high) * scale).astype(jnp.bfloat16)
    for block in range(8):
        factors_ref[block * 64 : 64 + block * 64] = sorted_rows[
            64:, block * 128 : (block + 1) * 128
        ]


def left_kernel(scale, outer_ref, factors_ref, right_ref, attn_ref, out_ref):
    right = jnp.concatenate(
        [factors_ref[block * 64 : 64 + block * 64] for block in range(8)], axis=1
    )
    sums = lax.dot_general(
        outer_ref[...], jnp.concatenate([right, jnp.zeros_like(right)], axis=0), NT,
        preferred_element_type=jnp.float32,
    ) * scale
    packed = right_ref[...].astype(jnp.float32)
    is_left = lax.broadcasted_iota(jnp.int32, (512, 128), 1) < 64
    low = jnp.where(is_left, sums[:512], pltpu.roll(packed, 64, 1)).astype(jnp.bfloat16)
    high = jnp.where(is_left, sums[512:], packed).astype(jnp.bfloat16)
    half = out_ref.shape[0] // 2
    for n in range(half):
        out_ref[n, :HALF] = low[n * HALF : (n + 1) * HALF]
        out_ref[n + half, :HALF] = high[n * HALF : (n + 1) * HALF]
    for n in range(2 * half):
        out_ref[n, HALF:] = attn_ref[n]


def call(kernel, shapes, specs, flops):
    many = isinstance(shapes, list)
    out = [jax.ShapeDtypeStruct(x, jnp.bfloat16) for x in (shapes if many else [shapes])]
    return pl.pallas_call(
        kernel,
        out_shape=out if many else out[0],
        in_specs=specs,
        out_specs=[VMEM] * len(out) if many else VMEM,
        compiler_params=pltpu.CompilerParams(vmem_limit_bytes=LIMIT),
        cost_estimate=pl.CostEstimate(flops=flops, bytes_accessed=4 << 20, transcendentals=0),
    )


def local(
    pair,
    first,
    second,
    incoming,
    acts,
    couple_map,
    half_map,
    qkvg_map,
    result_map,
):
    ni = lax.axis_size("ri")
    nj = lax.axis_size("rj")
    chips = nj // 2
    core = lax.axis_index("rj") % 2
    rows, cols, pair_features = pair.shape
    own_rows = incoming.shape[1]
    depth = own_rows * nj
    share = depth // 2
    features = incoming.shape[2]
    both = ("ri", "rj")
    wide = rows * HALF
    scale = 1.0 / depth

    halves = call(factors_kernel, (chips * 2 * own_rows, wide), [VMEM, VMEM], 1 << 27)(
        first, second
    )
    groups = [[2 * m + c for m in range(chips)] for c in range(2)]
    gathered = lax.all_to_all(
        halves.reshape(chips, 2 * own_rows, wide),
        "rj",
        0,
        0,
        axis_index_groups=groups,
        tiled=True,
    ).reshape(chips * 2 * own_rows, wide)

    other = lax.ppermute(pair, both, [(n, n ^ 1) for n in range(ni * nj)])
    outer_right = call(
        outer_right_kernel, (wide, wide), [SMEM, VMEM, VMEM, VMEM], 2 * 256 * 512 * 4096
    )(core.reshape(1), couple_map, pair, other)
    right_part, factors = call(
        functools.partial(right_kernel, scale), [(wide // 2, 128)] * 2, [VMEM, VMEM], 1 << 28
    )(outer_right, gathered)

    (pair, other, couple_map), right_part = lax.optimization_barrier(
        ((pair, other, couple_map), right_part)
    )
    places = [(p, m, c) for p in range(ni) for m in range(chips) for c in range(2)]
    factors = lax.ppermute(
        factors,
        both,
        [(m * nj + 2 * SOURCE[m][p] + c, p * nj + 2 * m + c) for p, m, c in places],
    )
    right_part = lax.ppermute(
        right_part,
        both,
        [(p * nj + 2 * m + c, m * nj + 2 * TARGET[m][p] + c) for p, m, c in places],
    )

    map_left = (
        couple_map.reshape(HALF, 8, 4, pair_features).transpose(1, 0, 2, 3).reshape(256, 512)
    )
    outer_left = call(
        outer_left_kernel, (wide, wide), [SMEM, VMEM, VMEM, VMEM], 2 * 256 * 512 * 4096
    )(core.reshape(1), map_left, pair, other)
    attn_in = jnp.concatenate(
        [acts.reshape(rows, 2 * own_rows, 128), incoming.reshape(rows, 2 * own_rows, 128)], axis=1
    )
    sums = call(
        functools.partial(left_kernel, scale), (rows, HALF + 16, 128), [VMEM] * 4, 1 << 28
    )(outer_left, factors, right_part, attn_in)
    received = lax.all_to_all(sums, "rj", 0, 0, tiled=True)
    sums = received[:, :HALF]
    acts_res = received[:, HALF : HALF + 8].reshape(depth, features)
    inc_res = received[:, HALF + 8 :].reshape(depth, features)
    sums = jnp.sum(
        sums.reshape(chips, 2, HALF, 2, share).astype(jnp.float32), axis=0
    ).astype(jnp.bfloat16)
    factor = (
        sums.reshape(2, HALF, 2, chips, own_rows)
        .transpose(2, 1, 3, 0, 4)
        .reshape(2 * HALF, depth)
    )
    grad = (
        inc_res.astype(jnp.float32)
        + jnp.einsum("fs,mf->sm", factor, half_map, preferred_element_type=jnp.float32)
    ).astype(jnp.bfloat16)
    result = attention_backward(acts_res, grad, qkvg_map, result_map)
    return lax.all_to_all(result.reshape(nj, own_rows, features), "rj", 0, 0, tiled=True)


def solution(mesh):
    return jax.shard_map(
        local,
        mesh=mesh,
        in_specs=(
            P("ri", "rj", None),
            P("ri", "rj"),
            P("ri", "rj"),
            P("ri", "rj", None),
            P("ri", "rj", None),
            P(),
            P(),
            P(),
            P(),
        ),
        out_specs=P("ri", "rj", None),
        check_vma=False,
    )
```

```python
import functools

import jax
import jax.numpy as jnp
from jax import lax
from jax.experimental import pallas as pl
from jax.experimental.pallas import tpu as pltpu
from jax.sharding import PartitionSpec as P

HALF = 32
HEADS = 8
NT = (((1,), (1,)), ((), ()))
VMEM = pl.BlockSpec(memory_space=pltpu.VMEM)
SMEM = pl.BlockSpec(memory_space=pltpu.SMEM)
LIMIT = 40 * 1024 * 1024
SOURCE = (
    (0, 3, 5, 4, 11, 10, 9, 14, 13, 15, 12, 8, 6, 7, 1, 2),
    (3, 2, 0, 1, 9, 15, 11, 10, 13, 8, 12, 14, 6, 7, 4, 5),
    (6, 7, 1, 2, 13, 11, 8, 9, 10, 15, 12, 14, 0, 3, 4, 5),
    (2, 3, 4, 1, 10, 11, 8, 9, 13, 14, 15, 12, 5, 7, 0, 6),
    (7, 6, 1, 2, 5, 11, 8, 4, 14, 15, 9, 10, 3, 0, 12, 13),
    (3, 8, 7, 0, 10, 5, 4, 6, 15, 12, 11, 9, 1, 2, 14, 13),
    (5, 3, 0, 4, 6, 7, 8, 10, 9, 11, 12, 13, 14, 15, 1, 2),
    (2, 4, 5, 1, 7, 8, 9, 6, 10, 11, 12, 13, 14, 15, 3, 0),
    (15, 12, 0, 1, 3, 2, 4, 5, 9, 10, 11, 8, 6, 7, 13, 14),
    (13, 14, 2, 1, 3, 4, 0, 6, 10, 11, 5, 9, 7, 12, 15, 8),
    (2, 3, 13, 14, 1, 6, 7, 0, 11, 4, 5, 10, 15, 8, 9, 12),
    (2, 3, 15, 12, 6, 7, 0, 1, 10, 11, 4, 5, 13, 14, 8, 9),
    (10, 12, 15, 13, 3, 2, 0, 1, 6, 7, 4, 5, 14, 11, 8, 9),
    (11, 15, 8, 10, 5, 3, 0, 1, 2, 6, 7, 4, 14, 13, 12, 9),
    (9, 11, 8, 12, 6, 7, 4, 5, 2, 0, 3, 1, 10, 15, 13, 14),
    (9, 14, 12, 13, 2, 3, 1, 0, 5, 4, 7, 6, 11, 10, 8, 15),
)
TARGET = (
    (0, 3, 5, 4, 11, 10, 9, 14, 13, 15, 12, 8, 6, 7, 1, 2),
    (3, 2, 0, 1, 9, 15, 11, 10, 13, 8, 12, 14, 6, 7, 4, 5),
    (6, 7, 1, 2, 13, 11, 8, 9, 10, 15, 12, 14, 0, 3, 4, 5),
    (2, 3, 4, 1, 10, 11, 8, 9, 13, 14, 15, 12, 5, 7, 0, 6),
    (7, 6, 1, 2, 5, 11, 8, 4, 14, 15, 9, 10, 3, 0, 12, 13),
    (3, 8, 7, 0, 10, 5, 4, 6, 15, 12, 11, 9, 1, 2, 14, 13),
    (5, 3, 0, 4, 6, 7, 8, 10, 9, 11, 12, 13, 14, 15, 1, 2),
    (2, 4, 5, 1, 7, 8, 9, 6, 10, 11, 12, 13, 14, 15, 3, 0),
    (15, 12, 0, 1, 3, 2, 4, 5, 9, 10, 11, 8, 6, 7, 13, 14),
    (13, 14, 2, 1, 3, 4, 0, 6, 10, 11, 5, 9, 7, 12, 15, 8),
    (2, 3, 13, 14, 1, 6, 7, 0, 11, 4, 5, 10, 15, 8, 9, 12),
    (2, 3, 15, 12, 6, 7, 0, 1, 10, 11, 4, 5, 13, 14, 8, 9),
    (10, 12, 15, 13, 3, 2, 0, 1, 6, 7, 4, 5, 14, 11, 8, 9),
    (11, 15, 8, 10, 5, 3, 0, 1, 2, 6, 7, 4, 14, 13, 12, 9),
    (9, 11, 8, 12, 6, 7, 4, 5, 2, 0, 3, 1, 10, 15, 13, 14),
    (9, 14, 12, 13, 2, 3, 1, 0, 5, 4, 7, 6, 11, 10, 8, 15),
)


def attention_backward(acts, grad, qkvg_map, result_map):
    rows, features = acts.shape
    head = features // HEADS
    scale = head ** (-0.5)
    projected = jnp.einsum(
        "cx,xy->cy", acts, qkvg_map, preferred_element_type=jnp.float32
    ).astype(jnp.bfloat16)
    shaped = projected.reshape(rows, 4, HEADS, head)
    queries, keys, values, logits = shaped[:, 0], shaped[:, 1], shaped[:, 2], shaped[:, 3]
    scores = jnp.einsum("shd,thd->hst", queries, keys, preferred_element_type=jnp.float32) * scale
    weights = jnp.exp(scores)
    attention = weights / jnp.sum(weights, axis=-1, keepdims=True)
    low = attention.astype(jnp.bfloat16)
    attended = jnp.einsum("hst,thd->shd", low, values, preferred_element_type=jnp.float32)
    gate = jax.nn.sigmoid(logits.astype(jnp.float32))
    grad_gated = jnp.einsum(
        "sm,om->so", grad, result_map, preferred_element_type=jnp.float32
    ).reshape(rows, HEADS, head)
    grad_attended = (gate * grad_gated).astype(jnp.bfloat16)
    grad_logits = grad_gated * attended * gate * (1.0 - gate)
    grad_weights = jnp.einsum(
        "shd,thd->hst", grad_attended, values, preferred_element_type=jnp.float32
    )
    grad_scores = (
        attention
        * (grad_weights - jnp.sum(attention * grad_weights, axis=-1, keepdims=True))
        * scale
    ).astype(jnp.bfloat16)
    grad_queries = jnp.einsum("hst,thd->shd", grad_scores, keys, preferred_element_type=jnp.float32)
    grad_keys = jnp.einsum("hst,shd->thd", grad_scores, queries, preferred_element_type=jnp.float32)
    grad_values = jnp.einsum("hst,shd->thd", low, grad_attended, preferred_element_type=jnp.float32)
    grad_projected = (
        jnp.stack([grad_queries, grad_keys, grad_values, grad_logits], axis=1)
        .reshape(rows, 4 * features)
        .astype(jnp.bfloat16)
    )
    back = jnp.einsum("sa,qa->sq", grad_projected, qkvg_map, preferred_element_type=jnp.float32)
    return (grad.astype(jnp.float32) + back).astype(jnp.bfloat16)


def outer_blocks(lhs, count, pieces, store):
    zero = jnp.zeros((HALF, 128), jnp.bfloat16)
    for n in range(count):
        stacked = []
        for piece in pieces:
            x = piece(n)
            for g in range(4):
                stacked.append(
                    jnp.concatenate([x if h == g else zero for h in range(4)], axis=1)
                )
        product = lax.dot_general(
            lhs, jnp.concatenate(stacked, axis=0), NT, preferred_element_type=jnp.float32
        ).astype(jnp.bfloat16)
        for m in range(len(pieces)):
            for g in range(8):
                store(
                    m, n, g, product[g * HALF : (g + 1) * HALF, m * 128 : (m + 1) * 128]
                )


def factors_kernel(first_ref, second_ref, out_ref):
    shape = (256, 1024)
    copies = jnp.where(
        lax.broadcasted_iota(jnp.int32, (HALF, 1024), 0)
        == (lax.broadcasted_iota(jnp.int32, (HALF, 1024), 1) & 31),
        1.0,
        0.0,
    ).astype(jnp.bfloat16)
    both = jnp.concatenate([first_ref[...], second_ref[...]], axis=1)
    tiled = lax.dot_general(
        both, copies, (((0,), (0,)), ((), ())), preferred_element_type=jnp.float32
    )
    own_channel = (lax.broadcasted_iota(jnp.int32, shape, 0) & 31) == (
        lax.broadcasted_iota(jnp.int32, shape, 1) >> 5
    )
    kept = jnp.where(own_channel, tiled, 0.0).astype(jnp.bfloat16)
    rows = jnp.where(
        (lax.broadcasted_iota(jnp.int32, (128, 256), 0) & 7)
        == (lax.broadcasted_iota(jnp.int32, (128, 256), 1) >> 5),
        1.0,
        0.0,
    ).astype(jnp.bfloat16)
    out_ref[...] = jnp.dot(rows, kept, preferred_element_type=jnp.float32).astype(jnp.bfloat16)


def outer_right_kernel(core_ref, map_ref, own_ref, other_ref, out_ref):
    lhs = jnp.concatenate(
        [
            jnp.concatenate(
                [map_ref[(h * 4 + g) * HALF : (h * 4 + g + 1) * HALF] for g in range(4)], axis=1
            )
            for h in range(8)
        ],
        axis=0,
    )
    cols = own_ref.shape[1]
    count = own_ref.shape[0] * cols
    to = lax.broadcasted_iota(jnp.int32, (count, count), 0)
    at = lax.broadcasted_iota(jnp.int32, (count, count), 1)
    order = jnp.where(at == (to & 31) * cols + (to >> 5), 1.0, 0.0).astype(jnp.bfloat16)
    turned = jnp.dot(
        order,
        jnp.concatenate(
            [own_ref[...].reshape(count, 128), other_ref[...].reshape(count, 128)], axis=1
        ),
        preferred_element_type=jnp.float32,
    ).astype(jnp.bfloat16)
    core = core_ref[0]
    starts = [core * (cols * HALF), (1 - core) * (cols * HALF)]

    def store(m, n, g, block):
        row = pl.multiple_of(starts[m] + n * HALF, HALF)
        out_ref[pl.ds(row, HALF), g * 128 : (g + 1) * 128] = block

    outer_blocks(
        lhs, cols, [lambda n: turned[n * HALF : (n + 1) * HALF, :128],
         lambda n: turned[n * HALF : (n + 1) * HALF, 128:]], store
    )


def outer_left_kernel(core_ref, lhs_ref, own_ref, other_ref, out_ref):
    half = own_ref.shape[0] // 2
    is_even = core_ref[0] == 0

    def columns(i):
        own, other = own_ref[i], other_ref[i]
        return jnp.concatenate(
            [jnp.where(is_even, own, other), jnp.where(is_even, other, own)], axis=0
        )

    def store(m, n, g, block):
        row = (m * half + n) * HALF
        out_ref[row : row + HALF, g * 128 : (g + 1) * 128] = block

    outer_blocks(lhs_ref[...], half, [columns, lambda n: columns(half + n)], store)


def right_kernel(scale, outer_ref, gathered_ref, out_ref, factors_ref):
    to = lax.broadcasted_iota(jnp.int32, (128, 128), 0)
    at = lax.broadcasted_iota(jnp.int32, (128, 128), 1)
    want = ((to & 63) >> 2) * 8 + (to >> 6) * 4 + (to & 3)
    order = jnp.where(at == want, 1.0, 0.0).astype(jnp.bfloat16)
    sorted_rows = jnp.dot(
        order, gathered_ref[...], preferred_element_type=jnp.float32
    ).astype(jnp.bfloat16)
    left = sorted_rows[:64]
    none = jnp.zeros_like(left)
    low = lax.dot_general(
        outer_ref[:512], jnp.concatenate([left, none], axis=0), NT,
        preferred_element_type=jnp.float32,
    )
    high = lax.dot_general(
        outer_ref[512:], jnp.concatenate([none, left], axis=0), NT,
        preferred_element_type=jnp.float32,
    )
    out_ref[...] = ((low + high) * scale).astype(jnp.bfloat16)
    for block in range(8):
        factors_ref[block * 64 : 64 + block * 64] = sorted_rows[
            64:, block * 128 : (block + 1) * 128
        ]


def left_kernel(scale, outer_ref, factors_ref, right_ref, out_ref):
    right = jnp.concatenate(
        [factors_ref[block * 64 : 64 + block * 64] for block in range(8)], axis=1
    )
    sums = lax.dot_general(
        outer_ref[...], jnp.concatenate([right, jnp.zeros_like(right)], axis=0), NT,
        preferred_element_type=jnp.float32,
    ) * scale
    packed = right_ref[...].astype(jnp.float32)
    is_left = lax.broadcasted_iota(jnp.int32, (512, 128), 1) < 64
    low = jnp.where(is_left, sums[:512], pltpu.roll(packed, 64, 1)).astype(jnp.bfloat16)
    high = jnp.where(is_left, sums[512:], packed).astype(jnp.bfloat16)
    half = out_ref.shape[0] // 2
    for n in range(half):
        out_ref[n, :HALF] = low[n * HALF : (n + 1) * HALF]
        out_ref[n + half, :HALF] = high[n * HALF : (n + 1) * HALF]


def call(kernel, shapes, specs, flops):
    many = isinstance(shapes, list)
    out = [jax.ShapeDtypeStruct(x, jnp.bfloat16) for x in (shapes if many else [shapes])]
    return pl.pallas_call(
        kernel,
        out_shape=out if many else out[0],
        in_specs=specs,
        out_specs=[VMEM] * len(out) if many else VMEM,
        compiler_params=pltpu.CompilerParams(vmem_limit_bytes=LIMIT),
        cost_estimate=pl.CostEstimate(flops=flops, bytes_accessed=4 << 20, transcendentals=0),
    )


def local(
    pair,
    first,
    second,
    incoming,
    acts,
    couple_map,
    half_map,
    qkvg_map,
    result_map,
):
    ni = lax.axis_size("ri")
    nj = lax.axis_size("rj")
    chips = nj // 2
    core = lax.axis_index("rj") % 2
    rows, cols, pair_features = pair.shape
    own_rows = incoming.shape[1]
    depth = own_rows * nj
    share = depth // 2
    features = incoming.shape[2]
    both = ("ri", "rj")
    wide = rows * HALF
    scale = 1.0 / depth

    halves = call(factors_kernel, (chips * 2 * own_rows, wide), [VMEM, VMEM], 1 << 27)(
        first, second
    )
    groups = [[2 * m + c for m in range(chips)] for c in range(2)]
    gathered = lax.all_to_all(
        halves.reshape(chips, 2 * own_rows, wide),
        "rj",
        0,
        0,
        axis_index_groups=groups,
        tiled=True,
    ).reshape(chips * 2 * own_rows, wide)

    other = lax.ppermute(pair, both, [(n, n ^ 1) for n in range(ni * nj)])
    outer_right = call(
        outer_right_kernel, (wide, wide), [SMEM, VMEM, VMEM, VMEM], 2 * 256 * 512 * 4096
    )(core.reshape(1), couple_map, pair, other)
    right_part, factors = call(
        functools.partial(right_kernel, scale), [(wide // 2, 128)] * 2, [VMEM, VMEM], 1 << 28
    )(outer_right, gathered)

    (pair, other, couple_map, acts, incoming), right_part = lax.optimization_barrier(
        ((pair, other, couple_map, acts, incoming), right_part)
    )
    places = [(p, m, c) for p in range(ni) for m in range(chips) for c in range(2)]
    factors = lax.ppermute(
        factors,
        both,
        [(m * nj + 2 * SOURCE[m][p] + c, p * nj + 2 * m + c) for p, m, c in places],
    )
    right_part = lax.ppermute(
        right_part,
        both,
        [(p * nj + 2 * m + c, m * nj + 2 * TARGET[m][p] + c) for p, m, c in places],
    )

    map_left = (
        couple_map.reshape(HALF, 8, 4, pair_features).transpose(1, 0, 2, 3).reshape(256, 512)
    )
    outer_left = call(
        outer_left_kernel, (wide, wide), [SMEM, VMEM, VMEM, VMEM], 1 << 33
    )(core.reshape(1), map_left, pair, other)
    attn_in = lax.all_to_all(
        jnp.concatenate([acts, incoming], axis=1), "rj", 0, 0, tiled=True
    )
    acts_res = attn_in[:, :own_rows].reshape(depth, features)
    inc_res = attn_in[:, own_rows:].reshape(depth, features)
    sums = call(
        functools.partial(left_kernel, scale), (rows, HALF, 128), [VMEM] * 3, 1 << 28
    )(outer_left, factors, right_part)
    sums = lax.all_to_all(sums, "rj", 0, 0, tiled=True)
    sums = jnp.sum(
        sums.reshape(chips, 2, HALF, 2, share).astype(jnp.float32), axis=0
    ).astype(jnp.bfloat16)
    factor = (
        sums.reshape(2, HALF, 2, chips, own_rows)
        .transpose(2, 1, 3, 0, 4)
        .reshape(2 * HALF, depth)
    )
    grad = (
        inc_res.astype(jnp.float32)
        + jnp.einsum("fs,mf->sm", factor, half_map, preferred_element_type=jnp.float32)
    ).astype(jnp.bfloat16)
    result = attention_backward(acts_res, grad, qkvg_map, result_map)
    return lax.all_to_all(result.reshape(nj, own_rows, features), "rj", 0, 0, tiled=True)


def solution(mesh):
    return jax.shard_map(
        local,
        mesh=mesh,
        in_specs=(
            P("ri", "rj", None),
            P("ri", "rj"),
            P("ri", "rj"),
            P("ri", "rj", None),
            P("ri", "rj", None),
            P(),
            P(),
            P(),
            P(),
        ),
        out_specs=P("ri", "rj", None),
        check_vma=False,
    )
```
